128 devices in a mesh: wide: 16 (over x, y_hi, core), narrow: 8 (over y_lo, z).
Axes of the slice: x: 4, y: 4 (y_hi: 2, y_lo: 2; y = y_hi * 2 + y_lo), z: 4, core: 2. Of those that a mesh axis runs over, the one named last changes fastest.
Arguments:
- field: float32 [20, 256, 256, 256], P(None, 'wide', 'narrow'), may hold values from -6 to 6
- spec_weight: float32 [1, 2, 20, 20, 48, 1152], P(None, None, None, None, 'wide', 'narrow'), may hold values from -8 to 8
- lin_weight: float32 [1, 20, 20], replicated, may hold values from -1.25 to 1.25
- bias: float32 [1, 20], replicated, may hold values from -3 to 3
Outputs:
- result: float32 [20, 256, 256, 256], P(None, 'wide', 'narrow')
The draws below stay inside these ranges and needn't reach their ends.
All inputs are finite; a program needn't handle non-finite values.
Results may differ from the reference program's by a relative error of at most 0.0001.
Values sent between devices are 32-bit elements; how exact they have to be, the bound alone decides.
No kernel may reach another device: no remote copies, remote signals or barrier semaphores. Data moves between devices by JAX's collectives and lax.ppermute only.
A program may use at most 128 MiB of HBM per device.

```python
import jax
import jax.numpy as jnp
from jax import lax

N = 256
C = 20
MX = 48
MY = 48
MZ = 24
LAYERS = 1


def shard_levels(own_key, dims, split, smallest, top_value):
    factor_of = 1.0
    for position, shards_of in split:
        heights = jax.random.uniform(jax.random.fold_in(jax.random.fold_in(own_key, 6), position), (shards_of,), jnp.float32, smallest / len(split), top_value / len(split))
        factor_of = factor_of * jnp.repeat(jnp.exp(heights), dims[position] // shards_of).reshape((-1,) + (1,) * (len(dims) - 1 - position))
    return factor_of


def bell_draw(stream_key, extent, scale, reach, pieces=(), kind=jnp.bfloat16):
    factor_of = shard_levels(stream_key, extent, pieces, -0.22, 0.18) if pieces else 1.0
    array = jax.random.normal(stream_key, extent, jnp.float32) * scale * factor_of
    return jnp.minimum(jnp.maximum(array, -reach), reach).astype(kind)


def setup_inputs(seed: int = 0) -> dict:
    seeds = jax.random.split(jax.random.key(seed), 5)
    field = bell_draw(seeds[0], (C, N, N, N), 1.0, 6.0, ((1, 16), (2, 8)), jnp.float32)
    spec_weight = bell_draw(seeds[1], (LAYERS, 2, C, C, MX, MY * MZ), 2.0, 8.0, ((4, 16), (5, 8)), jnp.float32)
    lin_weight = bell_draw(seeds[2], (LAYERS, C, C), C ** -0.5, 1.25, (), jnp.float32)
    bias = bell_draw(seeds[3], (LAYERS, C), 0.5, 3.0, (), jnp.float32)
    return dict(field=field, spec_weight=spec_weight, lin_weight=lin_weight, bias=bias)


def forward_modes(plane):
    spec = jnp.fft.rfft(plane, axis=1)[:, :MZ, :]
    spec = jnp.fft.fft(spec, axis=2)
    spec = jnp.concatenate([spec[:, :, :MX // 2], spec[:, :, N - MX // 2:]], axis=2)
    spec = jnp.fft.fft(spec, axis=0)
    spec = jnp.concatenate([spec[:MY // 2], spec[N - MY // 2:]], axis=0)
    return spec


def backward_modes(spec):
    half_y = MY // 2
    padded = jnp.concatenate([spec[:half_y], jnp.zeros((N - MY, MZ, MX), spec.dtype), spec[half_y:]], axis=0)
    padded = jnp.fft.ifft(padded, axis=0)
    half_x = MX // 2
    padded = jnp.concatenate([padded[:, :, :half_x], jnp.zeros((N, MZ, N - MX), spec.dtype), padded[:, :, half_x:]], axis=2)
    padded = jnp.fft.ifft(padded, axis=2)
    return jnp.fft.irfft(padded, n=N, axis=1)


def reference(field, spec_weight, lin_weight, bias):
    hidden = field
    for layer in range(LAYERS):
        spectra = lax.map(forward_modes, hidden)
        weights = spec_weight[layer]
        complex_weight = (weights[0] + 1j * weights[1]).reshape(C, C, MX, MY, MZ)
        mixed = jnp.einsum('iyzx,ioxyz->oyzx', spectra, complex_weight)
        spatial = lax.map(backward_modes, mixed)
        linear = jnp.einsum('io,iyzx->oyzx', lin_weight[layer], hidden, precision=lax.Precision.HIGHEST)
        linear = linear + bias[layer][:, None, None, None]
        hidden = jax.nn.gelu(spatial + linear, approximate=False)
    return hidden
```

```python
import functools

import jax
import jax.numpy as jnp
import ml_dtypes
import numpy as np
from jax import lax
from jax.experimental import pallas as pl
from jax.experimental.pallas import tpu as pltpu
from jax.sharding import PartitionSpec as P

N = 256
C = 20
MX = 48
MY = 48
MZ = 24
WIDE = 16
NARROW = 8
HALF = 24
SEQS = 49
GROUPS = 4
LANES = GROUPS * 128
ROWS = 40

f32 = jnp.float32
bf16 = jnp.bfloat16


def signed(count):
    half = count // 2
    return np.concatenate([np.arange(half), np.arange(half) - half])


def halves(table):
    high = table.astype(ml_dtypes.bfloat16)
    low = (table - high.astype(np.float64)).astype(ml_dtypes.bfloat16)
    return high, low


def x_table():
    angle = 2 * np.pi * (np.outer(np.arange(HALF + 1), np.arange(N)) % N) / N
    table = np.zeros((64, N))
    table[: HALF + 1] = np.cos(angle)
    table[HALF + 1 : SEQS] = np.sin(angle[1:])
    return table


def z_tables(scale):
    angle = 2 * np.pi * np.outer(np.arange(32), np.arange(MZ)) / N
    table = np.zeros((GROUPS, 256, 2, 128))
    for group in range(GROUPS):
        for channel in range(5):
            rows = slice(32 * group + 32 * channel, 32 * group + 32 * channel + 32)
            lanes = slice(MZ * channel, MZ * channel + MZ)
            table[group, rows, 0, lanes] = np.cos(angle) * scale
            table[group, rows, 1, lanes] = np.sin(angle) * scale
    return table


def phase_table():
    angle = 2 * np.pi * (np.outer(np.arange(NARROW), np.arange(MZ)) % 8) / 8
    table = np.zeros((NARROW, 2, 128), np.float32)
    for channel in range(5):
        table[:, 0, MZ * channel : MZ * channel + MZ] = np.cos(angle)
        table[:, 1, MZ * channel : MZ * channel + MZ] = np.sin(angle)
    return table


def y_tables():
    angle = 2 * np.pi * (np.outer(signed(MY), np.arange(N)) % N) / N
    cosine = np.cos(angle).reshape(NARROW, 6, WIDE, 2, 8)
    sine = np.sin(angle).reshape(NARROW, 6, WIDE, 2, 8)
    forward = np.zeros((NARROW, ROWS, WIDE, 2, 3, 2, 8))
    backward = np.zeros((WIDE, 2, 3, 2, 8, NARROW, ROWS))
    for ky in range(6):
        for kx in range(3):
            real, imag = 6 * ky + kx, 6 * ky + 3 + kx
            c, s = cosine[:, ky], sine[:, ky]
            forward[:, real, :, :, kx, 0] = c
            forward[:, real, :, :, kx, 1] = s
            forward[:, imag, :, :, kx, 0] = -s
            forward[:, imag, :, :, kx, 1] = c
            c, s = (np.moveaxis(t, 0, -1) / N for t in (c, s))
            backward[:, :, kx, 0, :, :, real] = c
            backward[:, :, kx, 0, :, :, imag] = -s
            backward[:, :, kx, 1, :, :, real] = s
            backward[:, :, kx, 1, :, :, imag] = c
    return (
        forward.reshape(NARROW * ROWS, WIDE * 96),
        backward.reshape(WIDE * 96, NARROW * ROWS),
    )


def split(value):
    high = value.astype(bf16)
    return high, (value - high.astype(f32)).astype(bf16)


def dot(left, right, contract=((1,), (0,))):
    return lax.dot_general(left, right, (contract, ((), ())), preferred_element_type=f32)


def dot3(left, right):
    return dot(left[0], right[0]) + dot(left[0], right[1]) + dot(left[1], right[0])


def forward_cells(x_ref, e_ref, zh_ref, zl_ref, phase_ref, out_ref, seq_ref):
    row = lax.rem(pl.program_id(0), 8)
    high, low = split(x_ref[...].reshape(C * 32, N))
    both = dot(e_ref[...], high, ((1,), (1,)))
    seqs = both[:56] + both[64:120] + dot(e_ref[:64], low, ((1,), (1,)))[:56]
    for tile in range(5):
        seq_ref[tile, pl.ds(row, 56, stride=8), :] = seqs[:, 128 * tile : 128 * tile + 128]

    @pl.when(row == 7)
    def _():
        turn = phase_ref[lax.axis_index("narrow")]
        turn_c, turn_s = turn[0:1], turn[1:2]
        for group in range(GROUPS):
            window = jnp.concatenate(
                [seq_ref[group, : SEQS * 8, :], seq_ref[group + 1, : SEQS * 8, :]], axis=1
            )
            modes = dot3(split(window), (zh_ref[group], zl_ref[group]))
            cosine, sine = modes[:, :128], modes[:, 128:]
            cosine, sine = turn_c * cosine - turn_s * sine, turn_s * cosine + turn_c * sine
            lanes = slice(128 * group, 128 * group + 128)
            for index in range(MX):
                freq = index if index < 24 else 48 - index
                at = slice(8 * freq, 8 * freq + 8)
                real, imag = cosine[at], -sine[at]
                if freq:
                    at = slice(8 * (24 + freq), 8 * (24 + freq) + 8)
                    if index < 24:
                        real, imag = real - sine[at], imag - cosine[at]
                    else:
                        real, imag = real + sine[at], imag + cosine[at]
                kx = 16 * (index % 3)
                out_ref[index // 3, kx : kx + 8, lanes] = real
                out_ref[index // 3, kx + 8 : kx + 16, lanes] = imag


def forward_rows(high_ref, low_ref, in_ref, out_ref):
    step = pl.program_id(0)
    part = dot3((high_ref[...], low_ref[...]), split(in_ref[...].reshape(-1, LANES)))
    part = part.reshape(NARROW, ROWS, LANES)

    @pl.when(step == 0)
    def _():
        out_ref[...] = part

    @pl.when(step > 0)
    def _():
        out_ref[...] += part


def mix(in_ref, w_ref, out_ref):
    total = jnp.sum(in_ref[...], axis=0)
    lane = lax.broadcasted_iota(jnp.int32, (8, 128), 1)
    rows = [total[6 * ky : 6 * ky + 8] for ky in range(5)]
    rows.append(jnp.concatenate([total[30:36], total[30:32]], axis=0))

    def roll(value, shift):
        shift = shift % 128
        return pltpu.roll(value, shift, 1) if shift else value

    spectra = []
    for channel in range(C):
        group, place = divmod(channel, 5)
        first = jnp.zeros((8, 128), f32)
        for ky in range(6):
            block = roll(rows[ky][:, 128 * group : 128 * group + 128], MZ * (ky - place))
            first = jnp.where(lane >= MZ * ky, block, first)
        spectra.append(jnp.concatenate([first, block], axis=1)[:, :144])
    mixed = []
    for start in range(0, C, 5):
        real = jnp.zeros((5, 3, 144), f32)
        imag = jnp.zeros((5, 3, 144), f32)
        for channel in range(C):
            a, b = spectra[channel][None, 0:3], spectra[channel][None, 3:6]
            u = w_ref[0, channel, start : start + 5]
            v = w_ref[1, channel, start : start + 5]
            real += a * u - b * v
            imag += a * v + b * u
        for place in range(5):
            mixed.append(jnp.concatenate([real[place], imag[place]], axis=0))
    lane = lane[:6]
    for group in range(GROUPS):
        for ky in range(6):
            tile = jnp.zeros((6, 128), f32)
            for place in range(5):
                value = mixed[5 * group + place]
                block = value[:, :128]
                if ky == 5:
                    rest = jnp.concatenate([value[:, 128:], jnp.zeros((6, 112), f32)], axis=1)
                    block = jnp.where(lane >= 120, block, rest)
                block = roll(block, MZ * (place - ky))
                inside = (lane >= MZ * place) & (lane < MZ * place + MZ)
                tile = jnp.where(inside, block, tile)
            for narrow in range(NARROW):
                out_ref[narrow, 6 * ky : 6 * ky + 6, 128 * group : 128 * group + 128] = tile
    for narrow in range(NARROW):
        out_ref[narrow, 36:40, :] = jnp.zeros((4, LANES), f32)


def backward_rows(high_ref, low_ref, in_ref, out_ref):
    part = dot3((high_ref[...], low_ref[...]), split(in_ref[...].reshape(-1, LANES)))
    out_ref[...] = part.reshape(out_ref.shape)


def gelu(value):
    return 0.5 * value * (1.0 + lax.erf(value * np.float32(np.sqrt(0.5))))


def backward_cells(
    x_ref, in_ref, eh_ref, el_ref, zh_ref, zl_ref, phase_ref, lin_ref, bias_ref, out_ref, cell_ref, lh_ref, ll_ref
):
    step = pl.program_id(0)
    row = lax.rem(step, 8)

    @pl.when(step == 0)
    def _():
        spread = lax.broadcasted_iota(jnp.int32, (160, C), 0) // 8
        spread = (spread == lax.broadcasted_iota(jnp.int32, (160, C), 1)).astype(bf16)
        rows = lax.broadcasted_iota(jnp.int32, (160, 160), 0)
        cols = lax.broadcasted_iota(jnp.int32, (160, 160), 1)
        same = (rows & 7) == (cols & 7)
        for part, ref in zip(split(lin_ref[...]), (lh_ref, ll_ref)):
            wide = dot(spread, part, ((1,), (1,))).astype(bf16)
            wide = dot(wide, spread, ((1,), (1,)))
            ref[...] = jnp.where(same, wide, 0.0).astype(bf16)

    @pl.when(row == 0)
    def _():
        base = 48 * (step // 8)
        turn = phase_ref[lax.axis_index("narrow")]
        turn_c, turn_s = turn[0:1], turn[1:2]
        carry = None
        for group in range(GROUPS):
            lanes = slice(128 * group, 128 * group + 128)

            def mode(index, part):
                at = base + 16 * (index % 3) + 8 * part
                return in_ref[index // 3, pl.ds(pl.multiple_of(at, 8), 8), lanes]

            first, second = [], []
            for freq in range(HALF + 1):
                if freq == 0:
                    u, v = mode(0, 0), mode(0, 1)
                elif freq == HALF:
                    u, v = mode(48 - freq, 0), mode(48 - freq, 1)
                else:
                    u = mode(freq, 0) + mode(48 - freq, 0)
                    v = mode(freq, 1) + mode(48 - freq, 1)
                first.append(u)
                second.append(v)
            for freq in range(1, HALF + 1):
                if freq == HALF:
                    u, v = mode(48 - freq, 1), -mode(48 - freq, 0)
                else:
                    u = mode(48 - freq, 1) - mode(freq, 1)
                    v = mode(freq, 0) - mode(48 - freq, 0)
                first.append(u)
                second.append(v)
            u, v = jnp.concatenate(first, axis=0), jnp.concatenate(second, axis=0)
            u, v = turn_c * u - turn_s * v, turn_s * u + turn_c * v
            cells = dot3(split(jnp.concatenate([u, v], axis=1)), (zh_ref[group], zl_ref[group]))
            left, right = cells[:, :128], cells[:, 128:]
            cell_ref[group, : SEQS * 8, :] = left if carry is None else left + carry
            carry = right
        cell_ref[GROUPS, : SEQS * 8, :] = carry
        for tile in range(5):
            cell_ref[tile, SEQS * 8 :, :] = jnp.zeros((512 - SEQS * 8, 128), f32)

    seqs = jnp.concatenate(
        [cell_ref[tile, pl.ds(row, 64, stride=8), :] for tile in range(5)], axis=1
    )
    seqs = jnp.transpose(seqs)
    high, low = split(seqs)
    spatial = dot(high, eh_ref[...]) + dot(high, el_ref[...]) + dot(low, eh_ref[...])
    spatial = spatial.reshape(C, 32, N)
    for block in range(4):
        at = slice(8 * block, 8 * block + 8)
        high, low = split(x_ref[:, 0, at, :].reshape(C * 8, N))
        linear = dot(lh_ref[...], high) + dot(ll_ref[...], high) + dot(lh_ref[...], low)
        linear = linear.reshape(C, 8, N) + spatial[:, at]
        for channel in range(C):
            out_ref[channel, 0, at, :] = gelu(linear[channel] + bias_ref[0, channel])


def whole(shape):
    return pl.BlockSpec(shape, lambda *_: (0,) * len(shape))


def params(mib):
    return pltpu.CompilerParams(
        dimension_semantics=("arbitrary",), vmem_limit_bytes=mib * 1024 * 1024
    )


def body(field, spec_weight, lin_weight, bias):
    eh, el = halves(x_table())
    zh, zl = (t.reshape(GROUPS, 256, 256) for t in halves(z_tables(1.0)))
    phase = phase_table()
    cells = pl.pallas_call(
        forward_cells,
        grid=(16,),
        in_specs=[
            pl.BlockSpec((C, 1, 32, N), lambda y: (0, y, 0, 0)),
            whole((128, N)),
            whole((GROUPS, 256, 256)),
            whole((GROUPS, 256, 256)),
            whole((NARROW, 2, 128)),
        ],
        out_specs=pl.BlockSpec((WIDE, 48, LANES), lambda y: (0, y // 8, 0)),
        out_shape=jax.ShapeDtypeStruct((WIDE, 96, LANES), f32),
        scratch_shapes=[pltpu.VMEM((5, 512, 128), f32)],
        compiler_params=params(48),
        name="forward_cells",
    )(field, np.concatenate([eh, el]), zh, zl, phase)
    moved = lax.all_to_all(cells, "wide", split_axis=0, concat_axis=0, tiled=True)

    forward, backward = y_tables()
    forward, backward = halves(forward), halves(backward)
    rows = pl.pallas_call(
        forward_rows,
        grid=(4,),
        in_specs=[
            pl.BlockSpec((NARROW * ROWS, 384), lambda s: (0, s)),
            pl.BlockSpec((NARROW * ROWS, 384), lambda s: (0, s)),
            pl.BlockSpec((4, 96, LANES), lambda s: (s, 0, 0)),
        ],
        out_specs=whole((NARROW, ROWS, LANES)),
        out_shape=jax.ShapeDtypeStruct((NARROW, ROWS, LANES), f32),
        compiler_params=params(32),
        name="forward_rows",
    )(*forward, moved)
    moved = lax.all_to_all(rows, "narrow", split_axis=0, concat_axis=0, tiled=True)

    modes = pl.pallas_call(
        mix,
        out_shape=jax.ShapeDtypeStruct((NARROW, ROWS, LANES), f32),
        compiler_params=pltpu.CompilerParams(vmem_limit_bytes=32 * 1024 * 1024),
        name="mix",
    )(moved, spec_weight.reshape(2, C, C, 3, 144))
    moved = lax.all_to_all(modes, "narrow", split_axis=0, concat_axis=0, tiled=True)

    rows = pl.pallas_call(
        backward_rows,
        grid=(4,),
        in_specs=[
            pl.BlockSpec((384, NARROW * ROWS), lambda s: (s, 0)),
            pl.BlockSpec((384, NARROW * ROWS), lambda s: (s, 0)),
            whole((NARROW, ROWS, LANES)),
        ],
        out_specs=pl.BlockSpec((4, 96, LANES), lambda s: (s, 0, 0)),
        out_shape=jax.ShapeDtypeStruct((WIDE, 96, LANES), f32),
        compiler_params=params(32),
        name="backward_rows",
    )(*backward, moved)
    moved = lax.all_to_all(rows, "wide", split_axis=0, concat_axis=0, tiled=True)

    eh, el = halves(x_table() / N)
    scale = np.where(np.arange(MZ) == 0, 1.0, 2.0) / N
    table = z_tables(scale)
    table[:, :, 1] *= -1
    zh, zl = halves(table.reshape(GROUPS, 256, 256).transpose(0, 2, 1))
    return pl.pallas_call(
        backward_cells,
        grid=(16,),
        in_specs=[
            pl.BlockSpec((C, 1, 32, N), lambda y: (0, y, 0, 0)),
            whole((WIDE, 96, LANES)),
            whole((64, N)),
            whole((64, N)),
            whole((GROUPS, 256, 256)),
            whole((GROUPS, 256, 256)),
            whole((NARROW, 2, 128)),
            whole((C, C)),
            pl.BlockSpec(memory_space=pltpu.SMEM),
        ],
        out_specs=pl.BlockSpec((C, 1, 32, N), lambda y: (0, y, 0, 0)),
        out_shape=jax.ShapeDtypeStruct(field.shape, f32),
        scratch_shapes=[
            pltpu.VMEM((5, 512, 128), f32),
            pltpu.VMEM((160, 160), bf16),
            pltpu.VMEM((160, 160), bf16),
        ],
        compiler_params=params(48),
        name="backward_cells",
    )(field, moved, eh, el, zh, zl, phase, lin_weight.reshape(C, C), bias)


def solution(mesh):
    placed = (
        P(None, "wide", "narrow", None),
        P(None, None, None, None, "wide", "narrow"),
        P(),
        P(),
    )
    return jax.shard_map(
        body, mesh=mesh, in_specs=placed, out_specs=P(None, "wide", "narrow", None), check_vma=False
    )
```

```python
import functools

import jax
import jax.numpy as jnp
import ml_dtypes
import numpy as np
from jax import lax
from jax.experimental import pallas as pl
from jax.experimental.pallas import tpu as pltpu
from jax.sharding import PartitionSpec as P

N = 256
C = 20
MX = 48
MY = 48
MZ = 24
WIDE = 16
NARROW = 8
HALF = 24
SEQS = 49
GROUPS = 4
LANES = GROUPS * 128
ROWS = 40

f32 = jnp.float32
bf16 = jnp.bfloat16


def signed(count):
    half = count // 2
    return np.concatenate([np.arange(half), np.arange(half) - half])


def halves(table):
    high = table.astype(ml_dtypes.bfloat16)
    low = (table - high.astype(np.float64)).astype(ml_dtypes.bfloat16)
    return high, low


def x_table():
    angle = 2 * np.pi * (np.outer(np.arange(HALF + 1), np.arange(N)) % N) / N
    table = np.zeros((64, N))
    table[: HALF + 1] = np.cos(angle)
    table[HALF + 1 : SEQS] = np.sin(angle[1:])
    return table


def z_table(scale):
    angle = 2 * np.pi * np.outer(np.arange(32), np.arange(MZ)) / N
    table = np.zeros((352, 256))
    for channel in range(5):
        rows = slice(96 + 32 * channel, 128 + 32 * channel)
        lanes = MZ * channel
        table[rows, lanes : lanes + MZ] = np.cos(angle) * scale
        table[rows, 128 + lanes : 128 + lanes + MZ] = np.sin(angle) * scale
    return table


def window_of(ref, group):
    return ref[96 - 32 * group : 352 - 32 * group]


def phase_table():
    angle = 2 * np.pi * (np.outer(np.arange(NARROW), np.arange(MZ)) % 8) / 8
    table = np.zeros((NARROW, 2, 128), np.float32)
    for channel in range(5):
        table[:, 0, MZ * channel : MZ * channel + MZ] = np.cos(angle)
        table[:, 1, MZ * channel : MZ * channel + MZ] = np.sin(angle)
    return table


def y_tables():
    angle = 2 * np.pi * (np.outer(signed(MY), np.arange(N)) % N) / N
    cosine = np.cos(angle).reshape(NARROW, 6, WIDE, 2, 8)
    sine = np.sin(angle).reshape(NARROW, 6, WIDE, 2, 8)
    forward = np.zeros((NARROW, ROWS, WIDE, 2, 3, 2, 8))
    backward = np.zeros((WIDE, 2, 3, 2, 8, NARROW, ROWS))
    for ky in range(6):
        for kx in range(3):
            real, imag = 6 * ky + kx, 6 * ky + 3 + kx
            c, s = cosine[:, ky], sine[:, ky]
            forward[:, real, :, :, kx, 0] = c
            forward[:, real, :, :, kx, 1] = s
            forward[:, imag, :, :, kx, 0] = -s
            forward[:, imag, :, :, kx, 1] = c
            c, s = (np.moveaxis(t, 0, -1) / N for t in (c, s))
            backward[:, :, kx, 0, :, :, real] = c
            backward[:, :, kx, 0, :, :, imag] = -s
            backward[:, :, kx, 1, :, :, real] = s
            backward[:, :, kx, 1, :, :, imag] = c
    return (
        forward.reshape(NARROW * ROWS, WIDE * 96),
        backward.reshape(WIDE * 96, NARROW * ROWS),
    )


def split(value):
    high = value.astype(bf16)
    return high, (value - high.astype(f32)).astype(bf16)


def dot(left, right, contract=((1,), (0,))):
    return lax.dot_general(left, right, (contract, ((), ())), preferred_element_type=f32)


def dot3(left, right, contract=((1,), (0,))):
    return (
        dot(left[0], right[0], contract)
        + dot(left[0], right[1], contract)
        + dot(left[1], right[0], contract)
    )


def forward_cells(
    x_ref, e_ref, zh_ref, zl_ref, phase_ref, out_ref, x_buf, out_buf, seq_ref, in_sem, out_sem
):
    def fetch(y):
        return pltpu.make_async_copy(x_ref.at[:, y], x_buf.at[y], in_sem.at[y])

    def leave(half):
        at = pl.ds(48 * half, 48)
        return pltpu.make_async_copy(out_buf.at[:, at], out_ref.at[:, at], out_sem.at[half])

    for y in range(16):
        fetch(y).start()

    def half_step(half, carry):
        def row_step(row, carry):
            y = 8 * half + row
            fetch(y).wait()
            high, low = split(x_buf[y].reshape(C * 32, N))
            both = dot(e_ref[...], high, ((1,), (1,)))
            seqs = both[:56] + both[64:120] + dot(e_ref[:64], low, ((1,), (1,)))[:56]
            for tile in range(5):
                seq_ref[tile, pl.ds(row, 56, stride=8), :] = seqs[:, 128 * tile : 128 * tile + 128]
            return carry

        lax.fori_loop(0, 8, row_step, 0)
        base = pl.multiple_of(48 * half, 8)
        turn = phase_ref[lax.axis_index("narrow")]
        turn_c, turn_s = turn[0:1], turn[1:2]
        for group in range(GROUPS):
            window = jnp.concatenate(
                [seq_ref[group, : SEQS * 8, :], seq_ref[group + 1, : SEQS * 8, :]], axis=1
            )
            modes = dot3(split(window), (window_of(zh_ref, group), window_of(zl_ref, group)))
            cosine, sine = modes[:, :128], modes[:, 128:]
            cosine, sine = turn_c * cosine - turn_s * sine, turn_s * cosine + turn_c * sine
            lanes = slice(128 * group, 128 * group + 128)
            for index in range(MX):
                freq = index if index < 24 else 48 - index
                at = slice(8 * freq, 8 * freq + 8)
                real, imag = cosine[at], -sine[at]
                if freq:
                    at = slice(8 * (24 + freq), 8 * (24 + freq) + 8)
                    if index < 24:
                        real, imag = real - sine[at], imag - cosine[at]
                    else:
                        real, imag = real + sine[at], imag + cosine[at]
                kx = 16 * (index % 3)
                out_buf[index // 3, pl.ds(base + kx, 8), lanes] = real
                out_buf[index // 3, pl.ds(base + kx + 8, 8), lanes] = imag
        leave(half).start()
        return carry

    lax.fori_loop(0, 2, half_step, 0)
    for half in range(2):
        leave(half).wait()


def forward_rows(high_ref, low_ref, in_ref, out_ref):
    part = dot3((high_ref[...], low_ref[...]), split(in_ref[...].reshape(-1, LANES)))
    out_ref[...] = part.reshape(NARROW, ROWS, LANES)


def mix(in_ref, w_ref, out_ref):
    total = jnp.sum(in_ref[...], axis=0)
    lane = lax.broadcasted_iota(jnp.int32, (8, 128), 1)
    rows = [total[6 * ky : 6 * ky + 8] for ky in range(5)]
    rows.append(jnp.concatenate([total[30:36], total[30:32]], axis=0))

    def roll(value, shift):
        shift = shift % 128
        return pltpu.roll(value, shift, 1) if shift else value

    spectra = []
    for channel in range(C):
        group, place = divmod(channel, 5)
        first = jnp.zeros((8, 128), f32)
        for ky in range(6):
            block = roll(rows[ky][:, 128 * group : 128 * group + 128], MZ * (ky - place))
            first = jnp.where(lane >= MZ * ky, block, first)
        spectra.append(jnp.concatenate([first, block], axis=1)[:, :144])
    mixed = []
    for start in range(0, C, 5):
        real = jnp.zeros((5, 3, 144), f32)
        imag = jnp.zeros((5, 3, 144), f32)
        for channel in range(C):
            a, b = spectra[channel][None, 0:3], spectra[channel][None, 3:6]
            u = w_ref[0, channel, start : start + 5]
            v = w_ref[1, channel, start : start + 5]
            real += a * u - b * v
            imag += a * v + b * u
        for place in range(5):
            mixed.append(jnp.concatenate([real[place], imag[place]], axis=0))
    lane = lane[:6]
    for group in range(GROUPS):
        for ky in range(6):
            tile = jnp.zeros((6, 128), f32)
            for place in range(5):
                value = mixed[5 * group + place]
                block = value[:, :128]
                if ky == 5:
                    rest = jnp.concatenate([value[:, 128:], jnp.zeros((6, 112), f32)], axis=1)
                    block = jnp.where(lane >= 120, block, rest)
                block = roll(block, MZ * (place - ky))
                inside = (lane >= MZ * place) & (lane < MZ * place + MZ)
                tile = jnp.where(inside, block, tile)
            for narrow in range(NARROW):
                out_ref[narrow, 6 * ky : 6 * ky + 6, 128 * group : 128 * group + 128] = tile
    for narrow in range(NARROW):
        out_ref[narrow, 36:40, :] = jnp.zeros((4, LANES), f32)


def backward_rows(table_ref, in_ref, out_ref):
    high, low = split(in_ref[...].reshape(-1, LANES))
    part = dot(table_ref[...], jnp.concatenate([high, low, high], axis=0))
    out_ref[...] = part.reshape(out_ref.shape)


def gelu(value):
    return 0.5 * value * (1.0 + lax.erf(value * np.float32(np.sqrt(0.5))))


def linear_cells(
    x_ref, lin_ref, bias_ref, out_ref, x_buf, out_buf, lh_ref, ll_ref, in_sem, out_sem
):
    def fetch(y):
        return pltpu.make_async_copy(x_ref.at[:, y], x_buf.at[y], in_sem.at[y])

    def leave(y):
        return pltpu.make_async_copy(out_buf.at[y], out_ref.at[:, y], out_sem.at[y])

    for y in range(16):
        fetch(y).start()
    spread = lax.broadcasted_iota(jnp.int32, (160, C), 0) // 8
    spread = (spread == lax.broadcasted_iota(jnp.int32, (160, C), 1)).astype(bf16)
    rows = lax.broadcasted_iota(jnp.int32, (160, 160), 0)
    cols = lax.broadcasted_iota(jnp.int32, (160, 160), 1)
    same = (rows & 7) == (cols & 7)
    for part, ref in zip(split(lin_ref[...]), (lh_ref, ll_ref)):
        wide = dot(spread, part, ((1,), (1,))).astype(bf16)
        wide = dot(wide, spread, ((1,), (1,)))
        ref[...] = jnp.where(same, wide, 0.0).astype(bf16)

    def row_step(y, carry):
        fetch(y).wait()
        for block in range(4):
            at = slice(8 * block, 8 * block + 8)
            cells = split(x_buf[y, :, at, :].reshape(C * 8, N))
            linear = dot3((lh_ref[...], ll_ref[...]), cells).reshape(C, 8, N)
            for channel in range(C):
                out_buf[y, channel, at, :] = linear[channel] + bias_ref[0, channel]
        leave(y).start()
        return carry

    lax.fori_loop(0, 16, row_step, 0)
    for y in range(16):
        leave(y).wait()


def backward_cells(
    linear_ref, in_ref, e_ref, zh_ref, zl_ref, phase_ref, out_ref,
    x_buf, in_buf, out_buf, cell_ref, x_sem, in_sem, out_sem,
):
    def modes_in(half):
        at = pl.ds(48 * half, 48)
        return pltpu.make_async_copy(in_ref.at[:, at], in_buf.at[:, at], in_sem.at[half])

    def fetch(y):
        return pltpu.make_async_copy(linear_ref.at[:, y], x_buf.at[y], x_sem.at[y])

    def leave(y):
        return pltpu.make_async_copy(out_buf.at[y], out_ref.at[:, y], out_sem.at[y])

    for half in range(2):
        modes_in(half).start()
    for y in range(16):
        fetch(y).start()
    for tile in range(5):
        cell_ref[tile, SEQS * 8 :, :] = jnp.zeros((512 - SEQS * 8, 128), f32)

    def half_step(half, carry):
        modes_in(half).wait()
        base = 48 * half
        turn = phase_ref[lax.axis_index("narrow")]
        turn_c, turn_s = turn[0:1], turn[1:2]
        last = None
        for group in range(GROUPS):
            lanes = slice(128 * group, 128 * group + 128)

            def mode(index, part):
                at = base + 16 * (index % 3) + 8 * part
                return in_buf[index // 3, pl.ds(pl.multiple_of(at, 8), 8), lanes]

            first, second = [], []
            for freq in range(HALF + 1):
                if freq == 0:
                    u, v = mode(0, 0), mode(0, 1)
                elif freq == HALF:
                    u, v = mode(48 - freq, 0), mode(48 - freq, 1)
                else:
                    u = mode(freq, 0) + mode(48 - freq, 0)
                    v = mode(freq, 1) + mode(48 - freq, 1)
                first.append(u)
                second.append(v)
            for freq in range(1, HALF + 1):
                if freq == HALF:
                    u, v = mode(48 - freq, 1), -mode(48 - freq, 0)
                else:
                    u = mode(48 - freq, 1) - mode(freq, 1)
                    v = mode(freq, 0) - mode(48 - freq, 0)
                first.append(u)
                second.append(v)
            u, v = jnp.concatenate(first, axis=0), jnp.concatenate(second, axis=0)
            u, v = turn_c * u - turn_s * v, turn_s * u + turn_c * v
            cells = dot3(
                split(jnp.concatenate([u, v], axis=1)),
                (window_of(zh_ref, group), window_of(zl_ref, group)),
                ((1,), (1,)),
            )
            left, right = cells[:, :128], cells[:, 128:]
            cell_ref[group, : SEQS * 8, :] = left if last is None else left + last
            last = right
        cell_ref[GROUPS, : SEQS * 8, :] = last

        def row_step(row, carry):
            y = 8 * half + row
            seqs = jnp.concatenate(
                [cell_ref[tile, pl.ds(row, 64, stride=8), :] for tile in range(5)], axis=1
            )
            pair = jnp.transpose(jnp.concatenate(split(seqs), axis=0))
            spatial = dot(jnp.concatenate([pair, pair], axis=1), e_ref[...])
            fetch(y).wait()
            out_buf[y] = gelu(x_buf[y] + spatial.reshape(C, 32, N))
            leave(y).start()
            return carry

        lax.fori_loop(0, 8, row_step, 0)
        return carry

    lax.fori_loop(0, 2, half_step, 0)
    for y in range(16):
        leave(y).wait()


def whole(shape):
    return pl.BlockSpec(shape, lambda *_: (0,) * len(shape))


def params(mib):
    return pltpu.CompilerParams(
        dimension_semantics=("arbitrary",), vmem_limit_bytes=mib * 1024 * 1024
    )


def cells_forward(field):
    eh, el = halves(x_table())
    zh, zl = halves(z_table(1.0))
    vmem = pl.BlockSpec(memory_space=pltpu.VMEM)
    return pl.pallas_call(
        forward_cells,
        in_specs=[pl.BlockSpec(memory_space=pl.ANY), vmem, vmem, vmem, vmem],
        out_specs=pl.BlockSpec(memory_space=pl.ANY),
        out_shape=jax.ShapeDtypeStruct((WIDE, 96, LANES), f32),
        scratch_shapes=[
            pltpu.VMEM((16, C, 32, N), f32),
            pltpu.VMEM((WIDE, 96, LANES), f32),
            pltpu.VMEM((5, 512, 128), f32),
            pltpu.SemaphoreType.DMA((16,)),
            pltpu.SemaphoreType.DMA((2,)),
        ],
        compiler_params=pltpu.CompilerParams(vmem_limit_bytes=60 * 1024 * 1024),
        name="forward_cells",
    )(
        field,
        np.concatenate([eh, el]),
        zh,
        zl,
        phase_table(),
    )


def rows_forward(moved):
    high, low = halves(y_tables()[0])
    return pl.pallas_call(
        forward_rows,
        out_shape=jax.ShapeDtypeStruct((NARROW, ROWS, LANES), f32),
        compiler_params=pltpu.CompilerParams(vmem_limit_bytes=32 * 1024 * 1024),
        name="forward_rows",
    )(high, low, moved)


def mix_modes(moved, spec_weight):
    return pl.pallas_call(
        mix,
        out_shape=jax.ShapeDtypeStruct((NARROW, ROWS, LANES), f32),
        compiler_params=pltpu.CompilerParams(vmem_limit_bytes=32 * 1024 * 1024),
        name="mix",
    )(moved, spec_weight.reshape(2, C, C, 3, 144))


def rows_backward(moved):
    high, low = halves(y_tables()[1])
    return pl.pallas_call(
        backward_rows,
        grid=(2,),
        in_specs=[
            pl.BlockSpec((768, 3 * NARROW * ROWS), lambda s: (s, 0)),
            whole((NARROW, ROWS, LANES)),
        ],
        out_specs=pl.BlockSpec((8, 96, LANES), lambda s: (s, 0, 0)),
        out_shape=jax.ShapeDtypeStruct((WIDE, 96, LANES), f32),
        compiler_params=params(32),
        name="backward_rows",
    )(np.concatenate([high, high, low], axis=1), moved)


def linear_part(field, lin_weight, bias):
    return pl.pallas_call(
        linear_cells,
        in_specs=[
            pl.BlockSpec(memory_space=pl.ANY),
            pl.BlockSpec(memory_space=pltpu.VMEM),
            pl.BlockSpec(memory_space=pltpu.SMEM),
        ],
        out_specs=pl.BlockSpec(memory_space=pl.ANY),
        out_shape=jax.ShapeDtypeStruct(field.shape, f32),
        scratch_shapes=[
            pltpu.VMEM((16, C, 32, N), f32),
            pltpu.VMEM((16, C, 32, N), f32),
            pltpu.VMEM((160, 160), bf16),
            pltpu.VMEM((160, 160), bf16),
            pltpu.SemaphoreType.DMA((16,)),
            pltpu.SemaphoreType.DMA((16,)),
        ],
        compiler_params=pltpu.CompilerParams(vmem_limit_bytes=40 * 1024 * 1024),
        cost_estimate=pl.CostEstimate(
            flops=2 * 3 * 160 * field.size, bytes_accessed=8 * field.size, transcendentals=0
        ),
        name="linear_cells",
    )(field, lin_weight.reshape(C, C), bias)


def cells_backward(linear, moved):
    eh, el = halves(x_table() / N)
    scale = np.where(np.arange(MZ) == 0, 1.0, 2.0) / N
    table = z_table(scale)
    table[:, 128:] *= -1
    zh, zl = halves(table)
    vmem = pl.BlockSpec(memory_space=pltpu.VMEM)
    hbm = pl.BlockSpec(memory_space=pl.ANY)
    return pl.pallas_call(
        backward_cells,
        in_specs=[hbm, hbm, vmem, vmem, vmem, vmem],
        out_specs=hbm,
        out_shape=jax.ShapeDtypeStruct(linear.shape, f32),
        scratch_shapes=[
            pltpu.VMEM((16, C, 32, N), f32),
            pltpu.VMEM((WIDE, 96, LANES), f32),
            pltpu.VMEM((16, C, 32, N), f32),
            pltpu.VMEM((5, 512, 128), f32),
            pltpu.SemaphoreType.DMA((16,)),
            pltpu.SemaphoreType.DMA((2,)),
            pltpu.SemaphoreType.DMA((16,)),
        ],
        compiler_params=pltpu.CompilerParams(vmem_limit_bytes=60 * 1024 * 1024),
        name="backward_cells",
    )(linear, moved, np.concatenate([eh, eh, el, np.zeros_like(el)]), zh, zl, phase_table())


def body(field, spec_weight, lin_weight, bias):
    moved = cells_forward(field)
    moved = lax.all_to_all(moved, "wide", split_axis=0, concat_axis=0, tiled=True)
    moved = rows_forward(moved)
    moved = lax.all_to_all(moved, "narrow", split_axis=0, concat_axis=0, tiled=True)
    moved = mix_modes(moved, spec_weight)
    moved = lax.all_to_all(moved, "narrow", split_axis=0, concat_axis=0, tiled=True)
    moved = rows_backward(moved)
    moved = lax.all_to_all(moved, "wide", split_axis=0, concat_axis=0, tiled=True)
    linear = linear_part(field, lin_weight, bias)
    return cells_backward(linear, moved)


def solution(mesh):
    placed = (
        P(None, "wide", "narrow", None),
        P(None, None, None, None, "wide", "narrow"),
        P(),
        P(),
    )
    return jax.shard_map(
        body, mesh=mesh, in_specs=placed, out_specs=P(None, "wide", "narrow", None), check_vma=False
    )
```

```python
import functools

import jax
import jax.numpy as jnp
import ml_dtypes
import numpy as np
from jax import lax
from jax.experimental import pallas as pl
from jax.experimental.pallas import tpu as pltpu
from jax.sharding import PartitionSpec as P

N = 256
C = 20
MX = 48
MY = 48
MZ = 24
WIDE = 16
NARROW = 8
HALF = 24
SEQS = 49
GROUPS = 4
LANES = GROUPS * 128
AHEAD = 6
ROWS = 40

f32 = jnp.float32
bf16 = jnp.bfloat16


def signed(count):
    half = count // 2
    return np.concatenate([np.arange(half), np.arange(half) - half])


def halves(table):
    high = table.astype(ml_dtypes.bfloat16)
    low = (table - high.astype(np.float64)).astype(ml_dtypes.bfloat16)
    return high, low


def x_table():
    angle = 2 * np.pi * (np.outer(np.arange(HALF + 1), np.arange(N)) % N) / N
    table = np.zeros((64, N))
    table[: HALF + 1] = np.cos(angle)
    table[HALF + 1 : SEQS] = np.sin(angle[1:])
    return table


def z_table(scale):
    angle = 2 * np.pi * np.outer(np.arange(32), np.arange(MZ)) / N
    table = np.zeros((352, 256))
    for channel in range(5):
        rows = slice(96 + 32 * channel, 128 + 32 * channel)
        lanes = MZ * channel
        table[rows, lanes : lanes + MZ] = np.cos(angle) * scale
        table[rows, 128 + lanes : 128 + lanes + MZ] = np.sin(angle) * scale
    return table


def window_of(ref, group):
    return ref[96 - 32 * group : 352 - 32 * group]


def phase_table():
    angle = 2 * np.pi * (np.outer(np.arange(NARROW), np.arange(MZ)) % 8) / 8
    table = np.zeros((NARROW, 2, 128), np.float32)
    for channel in range(5):
        table[:, 0, MZ * channel : MZ * channel + MZ] = np.cos(angle)
        table[:, 1, MZ * channel : MZ * channel + MZ] = np.sin(angle)
    return table


def y_tables():
    angle = 2 * np.pi * (np.outer(signed(MY), np.arange(N)) % N) / N
    cosine = np.cos(angle).reshape(NARROW, 6, WIDE, 2, 8)
    sine = np.sin(angle).reshape(NARROW, 6, WIDE, 2, 8)
    forward = np.zeros((NARROW, ROWS, WIDE, 2, 3, 2, 8))
    backward = np.zeros((WIDE, 2, 3, 2, 8, NARROW, ROWS))
    for ky in range(6):
        for kx in range(3):
            real, imag = 6 * ky + kx, 6 * ky + 3 + kx
            c, s = cosine[:, ky], sine[:, ky]
            forward[:, real, :, :, kx, 0] = c
            forward[:, real, :, :, kx, 1] = s
            forward[:, imag, :, :, kx, 0] = -s
            forward[:, imag, :, :, kx, 1] = c
            c, s = (np.moveaxis(t, 0, -1) / N for t in (c, s))
            backward[:, :, kx, 0, :, :, real] = c
            backward[:, :, kx, 0, :, :, imag] = -s
            backward[:, :, kx, 1, :, :, real] = s
            backward[:, :, kx, 1, :, :, imag] = c
    return (
        forward.reshape(NARROW * ROWS, WIDE * 96),
        backward.reshape(WIDE * 96, NARROW * ROWS),
    )


def split(value):
    high = value.astype(bf16)
    return high, (value - high.astype(f32)).astype(bf16)


def dot(left, right, contract=((1,), (0,))):
    return lax.dot_general(left, right, (contract, ((), ())), preferred_element_type=f32)


def dot3(left, right, contract=((1,), (0,))):
    return (
        dot(left[0], right[0], contract)
        + dot(left[0], right[1], contract)
        + dot(left[1], right[0], contract)
    )


def forward_cells(
    x_ref, e_ref, zh_ref, zl_ref, phase_ref, out_ref, x_buf, out_buf, seq_ref, in_sem, out_sem
):
    def fetch(y):
        return pltpu.make_async_copy(x_ref.at[:, y], x_buf.at[y], in_sem.at[y])

    def leave(half):
        at = pl.ds(48 * half, 48)
        return pltpu.make_async_copy(out_buf.at[:, at], out_ref.at[:, at], out_sem.at[half])

    for y in range(AHEAD):
        fetch(y).start()

    def half_step(half, carry):
        def row_step(row, carry):
            y = 8 * half + row
            fetch(y).wait()

            @pl.when(y + AHEAD < 16)
            def _():
                fetch(y + AHEAD).start()

            high, low = split(x_buf[y].reshape(C * 32, N))
            both = dot(e_ref[...], high, ((1,), (1,)))
            seqs = both[:56] + both[64:120] + dot(e_ref[:64], low, ((1,), (1,)))[:56]
            for tile in range(5):
                seq_ref[tile, pl.ds(row, 56, stride=8), :] = seqs[:, 128 * tile : 128 * tile + 128]
            return carry

        lax.fori_loop(0, 8, row_step, 0)
        base = pl.multiple_of(48 * half, 8)
        turn = phase_ref[lax.axis_index("narrow")]
        turn_c, turn_s = turn[0:1], turn[1:2]
        for group in range(GROUPS):
            window = jnp.concatenate(
                [seq_ref[group, : SEQS * 8, :], seq_ref[group + 1, : SEQS * 8, :]], axis=1
            )
            modes = dot3(split(window), (window_of(zh_ref, group), window_of(zl_ref, group)))
            cosine, sine = modes[:, :128], modes[:, 128:]
            cosine, sine = turn_c * cosine - turn_s * sine, turn_s * cosine + turn_c * sine
            lanes = slice(128 * group, 128 * group + 128)
            for index in range(MX):
                freq = index if index < 24 else 48 - index
                at = slice(8 * freq, 8 * freq + 8)
                real, imag = cosine[at], -sine[at]
                if freq:
                    at = slice(8 * (24 + freq), 8 * (24 + freq) + 8)
                    if index < 24:
                        real, imag = real - sine[at], imag - cosine[at]
                    else:
                        real, imag = real + sine[at], imag + cosine[at]
                kx = 16 * (index % 3)
                out_buf[index // 3, pl.ds(base + kx, 8), lanes] = real
                out_buf[index // 3, pl.ds(base + kx + 8, 8), lanes] = imag
        leave(half).start()
        return carry

    lax.fori_loop(0, 2, half_step, 0)
    for half in range(2):
        leave(half).wait()


def forward_rows(high_ref, low_ref, in_ref, out_ref):
    part = dot3((high_ref[...], low_ref[...]), split(in_ref[...].reshape(-1, LANES)))
    out_ref[...] = part.reshape(NARROW, ROWS, LANES)


def arrange(w_ref, out_ref):
    out_ref[...] = jnp.zeros(out_ref.shape, f32)
    out_ref[:, :, 0:3, 0:144] = w_ref[0]
    out_ref[:, :, 3:6, 0:144] = w_ref[1]


def mix(in_ref, w_ref, out_ref):
    total = jnp.sum(in_ref[...], axis=0)
    lane = lax.broadcasted_iota(jnp.int32, (8, 128), 1)
    rows = [total[6 * ky : 6 * ky + 8] for ky in range(5)]
    rows.append(jnp.concatenate([total[30:36], total[30:32]], axis=0))

    def roll(value, shift):
        shift = shift % 128
        return pltpu.roll(value, shift, 1) if shift else value

    spectra = []
    for channel in range(C):
        group, place = divmod(channel, 5)
        first = jnp.zeros((8, 128), f32)
        for ky in range(6):
            block = roll(rows[ky][:, 128 * group : 128 * group + 128], MZ * (ky - place))
            first = jnp.where(lane >= MZ * ky, block, first)
        value = jnp.concatenate([first, block], axis=1)
        real, imag = value[0:3], value[3:6]
        spectra.append(
            (
                jnp.concatenate([real, real, real[0:2]], axis=0)[None],
                jnp.concatenate([imag, imag, imag[0:2]], axis=0)[None],
            )
        )
    mixed = []
    for start in range(0, C, 5):
        by_real = jnp.zeros((5, 8, 256), f32)
        by_imag = jnp.zeros((5, 8, 256), f32)
        for channel in range(C):
            weight = w_ref[channel, start : start + 5]
            by_real += spectra[channel][0] * weight
            by_imag += spectra[channel][1] * weight
        for place in range(5):
            real = by_real[place, 0:3] - by_imag[place, 3:6]
            imag = by_real[place, 3:6] + by_imag[place, 0:3]
            mixed.append(jnp.concatenate([real, imag], axis=0))
    lane = lane[:6]
    for group in range(GROUPS):
        for ky in range(6):
            tile = jnp.zeros((6, 128), f32)
            for place in range(5):
                value = mixed[5 * group + place]
                block = value[:, :128]
                if ky == 5:
                    rest = value[:, 128:]
                    block = jnp.where(lane >= 120, block, rest)
                block = roll(block, MZ * (place - ky))
                inside = (lane >= MZ * place) & (lane < MZ * place + MZ)
                tile = jnp.where(inside, block, tile)
            for narrow in range(NARROW):
                out_ref[narrow, 6 * ky : 6 * ky + 6, 128 * group : 128 * group + 128] = tile
    for narrow in range(NARROW):
        out_ref[narrow, 36:40, :] = jnp.zeros((4, LANES), f32)


def backward_rows(table_ref, in_ref, out_ref):
    high, low = split(in_ref[...].reshape(-1, LANES))
    part = dot(table_ref[...], jnp.concatenate([high, low, high], axis=0))
    out_ref[...] = part.reshape(out_ref.shape)


def gelu(value):
    return 0.5 * value * (1.0 + lax.erf(value * np.float32(np.sqrt(0.5))))


def linear_cells(
    x_ref, lin_ref, bias_ref, out_ref, x_buf, out_buf, lh_ref, ll_ref, in_sem, out_sem
):
    def fetch(y):
        return pltpu.make_async_copy(x_ref.at[:, y], x_buf.at[y], in_sem.at[y])

    def leave(y):
        return pltpu.make_async_copy(out_buf.at[y], out_ref.at[:, y], out_sem.at[y])

    for y in range(16):
        fetch(y).start()
    spread = lax.broadcasted_iota(jnp.int32, (160, C), 0) // 8
    spread = (spread == lax.broadcasted_iota(jnp.int32, (160, C), 1)).astype(bf16)
    rows = lax.broadcasted_iota(jnp.int32, (160, 160), 0)
    cols = lax.broadcasted_iota(jnp.int32, (160, 160), 1)
    same = (rows & 7) == (cols & 7)
    for part, ref in zip(split(lin_ref[...]), (lh_ref, ll_ref)):
        wide = dot(spread, part, ((1,), (1,))).astype(bf16)
        wide = dot(wide, spread, ((1,), (1,)))
        ref[...] = jnp.where(same, wide, 0.0).astype(bf16)

    def row_step(y, carry):
        fetch(y).wait()
        for block in range(4):
            at = slice(8 * block, 8 * block + 8)
            cells = split(x_buf[y, :, at, :].reshape(C * 8, N))
            linear = dot3((lh_ref[...], ll_ref[...]), cells).reshape(C, 8, N)
            for channel in range(C):
                out_buf[y, channel, at, :] = linear[channel] + bias_ref[0, channel]
        leave(y).start()
        return carry

    lax.fori_loop(0, 16, row_step, 0)
    for y in range(16):
        leave(y).wait()


def backward_cells(
    linear_ref, in_ref, e_ref, zh_ref, zl_ref, phase_ref, out_ref,
    x_buf, in_buf, out_buf, cell_ref, x_sem, in_sem, out_sem,
):
    def modes_in(half):
        at = pl.ds(48 * half, 48)
        return pltpu.make_async_copy(in_ref.at[:, at], in_buf.at[:, at], in_sem.at[half])

    def fetch(y):
        return pltpu.make_async_copy(linear_ref.at[:, y], x_buf.at[y], x_sem.at[y])

    def leave(y):
        return pltpu.make_async_copy(out_buf.at[y], out_ref.at[:, y], out_sem.at[y])

    modes_in(0).start()
    for tile in range(5):
        cell_ref[tile, SEQS * 8 :, :] = jnp.zeros((512 - SEQS * 8, 128), f32)

    def half_step(half, carry):
        modes_in(half).wait()

        @pl.when(half == 0)
        def _():
            for y in range(AHEAD):
                fetch(y).start()
            modes_in(1).start()

        base = 48 * half
        turn = phase_ref[lax.axis_index("narrow")]
        turn_c, turn_s = turn[0:1], turn[1:2]
        last = None
        for group in range(GROUPS):
            lanes = slice(128 * group, 128 * group + 128)

            def mode(index, part):
                at = base + 16 * (index % 3) + 8 * part
                return in_buf[index // 3, pl.ds(pl.multiple_of(at, 8), 8), lanes]

            first, second = [], []
            for freq in range(HALF + 1):
                if freq == 0:
                    u, v = mode(0, 0), mode(0, 1)
                elif freq == HALF:
                    u, v = mode(48 - freq, 0), mode(48 - freq, 1)
                else:
                    u = mode(freq, 0) + mode(48 - freq, 0)
                    v = mode(freq, 1) + mode(48 - freq, 1)
                first.append(u)
                second.append(v)
            for freq in range(1, HALF + 1):
                if freq == HALF:
                    u, v = mode(48 - freq, 1), -mode(48 - freq, 0)
                else:
                    u = mode(48 - freq, 1) - mode(freq, 1)
                    v = mode(freq, 0) - mode(48 - freq, 0)
                first.append(u)
                second.append(v)
            u, v = jnp.concatenate(first, axis=0), jnp.concatenate(second, axis=0)
            u, v = turn_c * u - turn_s * v, turn_s * u + turn_c * v
            cells = dot3(
                split(jnp.concatenate([u, v], axis=1)),
                (window_of(zh_ref, group), window_of(zl_ref, group)),
                ((1,), (1,)),
            )
            left, right = cells[:, :128], cells[:, 128:]
            cell_ref[group, : SEQS * 8, :] = left if last is None else left + last
            last = right
        cell_ref[GROUPS, : SEQS * 8, :] = last

        def row_step(row, carry):
            y = 8 * half + row
            seqs = jnp.concatenate(
                [cell_ref[tile, pl.ds(row, 64, stride=8), :] for tile in range(5)], axis=1
            )
            pair = jnp.transpose(jnp.concatenate(split(seqs), axis=0))
            spatial = dot(jnp.concatenate([pair, pair], axis=1), e_ref[...])
            fetch(y).wait()

            @pl.when(y + AHEAD < 16)
            def _():
                fetch(y + AHEAD).start()

            out_buf[y] = gelu(x_buf[y] + spatial.reshape(C, 32, N))
            leave(y).start()
            return carry

        lax.fori_loop(0, 8, row_step, 0)
        return carry

    lax.fori_loop(0, 2, half_step, 0)
    for y in range(16):
        leave(y).wait()


def whole(shape):
    return pl.BlockSpec(shape, lambda *_: (0,) * len(shape))


def params(mib):
    return pltpu.CompilerParams(
        dimension_semantics=("arbitrary",), vmem_limit_bytes=mib * 1024 * 1024
    )


def cells_forward(field):
    eh, el = halves(x_table())
    zh, zl = halves(z_table(1.0))
    vmem = pl.BlockSpec(memory_space=pltpu.VMEM)
    return pl.pallas_call(
        forward_cells,
        in_specs=[pl.BlockSpec(memory_space=pl.ANY), vmem, vmem, vmem, vmem],
        out_specs=pl.BlockSpec(memory_space=pl.ANY),
        out_shape=jax.ShapeDtypeStruct((WIDE, 96, LANES), f32),
        scratch_shapes=[
            pltpu.VMEM((16, C, 32, N), f32),
            pltpu.VMEM((WIDE, 96, LANES), f32),
            pltpu.VMEM((5, 512, 128), f32),
            pltpu.SemaphoreType.DMA((16,)),
            pltpu.SemaphoreType.DMA((2,)),
        ],
        compiler_params=pltpu.CompilerParams(vmem_limit_bytes=60 * 1024 * 1024),
        name="forward_cells",
    )(
        field,
        np.concatenate([eh, el]),
        zh,
        zl,
        phase_table(),
    )


def rows_forward(moved):
    high, low = halves(y_tables()[0])
    return pl.pallas_call(
        forward_rows,
        out_shape=jax.ShapeDtypeStruct((NARROW, ROWS, LANES), f32),
        compiler_params=pltpu.CompilerParams(vmem_limit_bytes=32 * 1024 * 1024),
        name="forward_rows",
    )(high, low, moved)


def arrange_weights(spec_weight):
    return pl.pallas_call(
        arrange,
        grid=(4,),
        in_specs=[pl.BlockSpec((2, 5, C, 3, 144), lambda i: (0, i, 0, 0, 0))],
        out_specs=pl.BlockSpec((5, C, 8, 256), lambda i: (i, 0, 0, 0)),
        out_shape=jax.ShapeDtypeStruct((C, C, 8, 256), f32),
        compiler_params=params(32),
        name="arrange",
    )(spec_weight.reshape(2, C, C, 3, 144))


def mix_modes(moved, weights):
    return pl.pallas_call(
        mix,
        out_shape=jax.ShapeDtypeStruct((NARROW, ROWS, LANES), f32),
        compiler_params=pltpu.CompilerParams(vmem_limit_bytes=32 * 1024 * 1024),
        name="mix",
    )(moved, weights)


def rows_backward(moved):
    high, low = halves(y_tables()[1])
    return pl.pallas_call(
        backward_rows,
        grid=(2,),
        in_specs=[
            pl.BlockSpec((768, 3 * NARROW * ROWS), lambda s: (s, 0)),
            whole((NARROW, ROWS, LANES)),
        ],
        out_specs=pl.BlockSpec((8, 96, LANES), lambda s: (s, 0, 0)),
        out_shape=jax.ShapeDtypeStruct((WIDE, 96, LANES), f32),
        compiler_params=params(32),
        name="backward_rows",
    )(np.concatenate([high, high, low], axis=1), moved)


def linear_part(field, lin_weight, bias):
    return pl.pallas_call(
        linear_cells,
        in_specs=[
            pl.BlockSpec(memory_space=pl.ANY),
            pl.BlockSpec(memory_space=pltpu.VMEM),
            pl.BlockSpec(memory_space=pltpu.SMEM),
        ],
        out_specs=pl.BlockSpec(memory_space=pl.ANY),
        out_shape=jax.ShapeDtypeStruct(field.shape, f32),
        scratch_shapes=[
            pltpu.VMEM((16, C, 32, N), f32),
            pltpu.VMEM((16, C, 32, N), f32),
            pltpu.VMEM((160, 160), bf16),
            pltpu.VMEM((160, 160), bf16),
            pltpu.SemaphoreType.DMA((16,)),
            pltpu.SemaphoreType.DMA((16,)),
        ],
        compiler_params=pltpu.CompilerParams(vmem_limit_bytes=40 * 1024 * 1024),
        cost_estimate=pl.CostEstimate(
            flops=2 * 3 * 160 * field.size, bytes_accessed=8 * field.size, transcendentals=0
        ),
        name="linear_cells",
    )(field, lin_weight.reshape(C, C), bias)


def cells_backward(linear, moved):
    eh, el = halves(x_table() / N)
    scale = np.where(np.arange(MZ) == 0, 1.0, 2.0) / N
    table = z_table(scale)
    table[:, 128:] *= -1
    zh, zl = halves(table)
    vmem = pl.BlockSpec(memory_space=pltpu.VMEM)
    hbm = pl.BlockSpec(memory_space=pl.ANY)
    return pl.pallas_call(
        backward_cells,
        in_specs=[hbm, hbm, vmem, vmem, vmem, vmem],
        out_specs=hbm,
        out_shape=jax.ShapeDtypeStruct(linear.shape, f32),
        scratch_shapes=[
            pltpu.VMEM((16, C, 32, N), f32),
            pltpu.VMEM((WIDE, 96, LANES), f32),
            pltpu.VMEM((16, C, 32, N), f32),
            pltpu.VMEM((5, 512, 128), f32),
            pltpu.SemaphoreType.DMA((16,)),
            pltpu.SemaphoreType.DMA((2,)),
            pltpu.SemaphoreType.DMA((16,)),
        ],
        compiler_params=pltpu.CompilerParams(vmem_limit_bytes=46 * 1024 * 1024),
        name="backward_cells",
    )(linear, moved, np.concatenate([eh, eh, el, np.zeros_like(el)]), zh, zl, phase_table())


def body(field, spec_weight, lin_weight, bias):
    moved = cells_forward(field)
    moved = lax.all_to_all(moved, "wide", split_axis=0, concat_axis=0, tiled=True)
    moved = rows_forward(moved)
    moved = lax.all_to_all(moved, "narrow", split_axis=0, concat_axis=0, tiled=True)
    moved = mix_modes(moved, arrange_weights(spec_weight))
    moved = lax.all_to_all(moved, "narrow", split_axis=0, concat_axis=0, tiled=True)
    moved = rows_backward(moved)
    moved = lax.all_to_all(moved, "wide", split_axis=0, concat_axis=0, tiled=True)
    linear = linear_part(field, lin_weight, bias)
    return cells_backward(linear, moved)


def solution(mesh):
    placed = (
        P(None, "wide", "narrow", None),
        P(None, None, None, None, "wide", "narrow"),
        P(),
        P(),
    )
    return jax.shard_map(
        body, mesh=mesh, in_specs=placed, out_specs=P(None, "wide", "narrow", None), check_vma=False
    )
```

```python
import functools

import jax
import jax.numpy as jnp
import ml_dtypes
import numpy as np
from jax import lax
from jax.experimental import pallas as pl
from jax.experimental.pallas import tpu as pltpu
from jax.sharding import PartitionSpec as P

N = 256
C = 20
MX = 48
MY = 48
MZ = 24
WIDE = 16
NARROW = 8
HALF = 24
SEQS = 49
GROUPS = 4
LANES = GROUPS * 128
AHEAD = 6
ROWS = 40

f32 = jnp.float32
bf16 = jnp.bfloat16


def signed(count):
    half = count // 2
    return np.concatenate([np.arange(half), np.arange(half) - half])


def halves(table):
    high = table.astype(ml_dtypes.bfloat16)
    low = (table - high.astype(np.float64)).astype(ml_dtypes.bfloat16)
    return high, low


def x_table():
    angle = 2 * np.pi * (np.outer(np.arange(HALF + 1), np.arange(N)) % N) / N
    table = np.zeros((64, N))
    table[: HALF + 1] = np.cos(angle)
    table[HALF + 1 : SEQS] = np.sin(angle[1:])
    return table


def z_table(scale):
    angle = 2 * np.pi * np.outer(np.arange(32), np.arange(MZ)) / N
    table = np.zeros((352, 256))
    for channel in range(5):
        rows = slice(96 + 32 * channel, 128 + 32 * channel)
        lanes = MZ * channel
        table[rows, lanes : lanes + MZ] = np.cos(angle) * scale
        table[rows, 128 + lanes : 128 + lanes + MZ] = np.sin(angle) * scale
    return table


def window_of(ref, group, base=0):
    return ref[base + 96 - 32 * group : base + 352 - 32 * group]


def phase_table():
    angle = 2 * np.pi * (np.outer(np.arange(NARROW), np.arange(MZ)) % 8) / 8
    table = np.zeros((NARROW, 2, 128), np.float32)
    for channel in range(5):
        table[:, 0, MZ * channel : MZ * channel + MZ] = np.cos(angle)
        table[:, 1, MZ * channel : MZ * channel + MZ] = np.sin(angle)
    return table


def y_tables():
    angle = 2 * np.pi * (np.outer(signed(MY), np.arange(N)) % N) / N
    cosine = np.cos(angle).reshape(NARROW, 6, WIDE, 2, 8)
    sine = np.sin(angle).reshape(NARROW, 6, WIDE, 2, 8)
    forward = np.zeros((NARROW, ROWS, WIDE, 2, 3, 2, 8))
    backward = np.zeros((WIDE, 2, 3, 2, 8, NARROW, ROWS))
    for ky in range(6):
        for kx in range(3):
            real, imag = 6 * ky + kx, 6 * ky + 3 + kx
            c, s = cosine[:, ky], sine[:, ky]
            forward[:, real, :, :, kx, 0] = c
            forward[:, real, :, :, kx, 1] = s
            forward[:, imag, :, :, kx, 0] = -s
            forward[:, imag, :, :, kx, 1] = c
            c, s = (np.moveaxis(t, 0, -1) / N for t in (c, s))
            backward[:, :, kx, 0, :, :, real] = c
            backward[:, :, kx, 0, :, :, imag] = -s
            backward[:, :, kx, 1, :, :, real] = s
            backward[:, :, kx, 1, :, :, imag] = c
    return (
        forward.reshape(NARROW * ROWS, WIDE * 96),
        backward.reshape(WIDE * 96, NARROW * ROWS),
    )


def split(value):
    high = value.astype(bf16)
    return high, (value - high.astype(f32)).astype(bf16)


def dot(left, right, contract=((1,), (0,))):
    return lax.dot_general(left, right, (contract, ((), ())), preferred_element_type=f32)


def dot3(left, right, contract=((1,), (0,))):
    return (
        dot(left[0], right[0], contract)
        + dot(left[0], right[1], contract)
        + dot(left[1], right[0], contract)
    )


def forward_cells(
    x_ref, e_ref, zh_ref, zl_ref, phase_ref, out_ref, x_buf, out_buf, seq_ref, in_sem, out_sem
):
    def fetch(y):
        return pltpu.make_async_copy(x_ref.at[:, y], x_buf.at[y], in_sem.at[y])

    def leave(half):
        at = pl.ds(48 * half, 48)
        return pltpu.make_async_copy(out_buf.at[:, at], out_ref.at[:, at], out_sem.at[half])

    for y in range(AHEAD):
        fetch(y).start()

    def half_step(half, carry):
        def row_step(row, carry):
            y = 8 * half + row
            fetch(y).wait()

            @pl.when(y + AHEAD < 16)
            def _():
                fetch(y + AHEAD).start()

            high, low = split(x_buf[y].reshape(C * 32, N))
            both = dot(e_ref[...], high, ((1,), (1,)))
            seqs = both[:56] + both[64:120] + dot(e_ref[:64], low, ((1,), (1,)))[:56]
            for tile in range(5):
                seq_ref[tile, pl.ds(row, 56, stride=8), :] = seqs[:, 128 * tile : 128 * tile + 128]
            return carry

        lax.fori_loop(0, 8, row_step, 0)
        base = pl.multiple_of(48 * half, 8)
        turn = phase_ref[lax.axis_index("narrow")]
        turn_c, turn_s = turn[0:1], turn[1:2]
        for group in range(GROUPS):
            window = jnp.concatenate(
                [seq_ref[group, : SEQS * 8, :], seq_ref[group + 1, : SEQS * 8, :]], axis=1
            )
            modes = dot3(split(window), (window_of(zh_ref, group), window_of(zl_ref, group)))
            cosine, sine = modes[:, :128], modes[:, 128:]
            cosine, sine = turn_c * cosine - turn_s * sine, turn_s * cosine + turn_c * sine
            lanes = slice(128 * group, 128 * group + 128)
            for index in range(MX):
                freq = index if index < 24 else 48 - index
                at = slice(8 * freq, 8 * freq + 8)
                real, imag = cosine[at], -sine[at]
                if freq:
                    at = slice(8 * (24 + freq), 8 * (24 + freq) + 8)
                    if index < 24:
                        real, imag = real - sine[at], imag - cosine[at]
                    else:
                        real, imag = real + sine[at], imag + cosine[at]
                kx = 16 * (index % 3)
                out_buf[index // 3, pl.ds(base + kx, 8), lanes] = real
                out_buf[index // 3, pl.ds(base + kx + 8, 8), lanes] = imag
        leave(half).start()
        return carry

    lax.fori_loop(0, 2, half_step, 0)
    for half in range(2):
        leave(half).wait()


def forward_rows(high_ref, low_ref, in_ref, out_ref):
    part = dot3((high_ref[...], low_ref[...]), split(in_ref[...].reshape(-1, LANES)))
    out_ref[...] = part.reshape(NARROW, ROWS, LANES)


def arrange(w_ref, out_ref):
    out_ref[...] = jnp.zeros(out_ref.shape, f32)
    out_ref[:, :, 0:3, 0:144] = w_ref[0]
    out_ref[:, :, 3:6, 0:144] = w_ref[1]


def mix(in_ref, w_ref, out_ref):
    total = jnp.sum(in_ref[...], axis=0)
    lane = lax.broadcasted_iota(jnp.int32, (8, 128), 1)
    rows = [total[6 * ky : 6 * ky + 8] for ky in range(5)]
    rows.append(jnp.concatenate([total[30:36], total[30:32]], axis=0))

    def roll(value, shift):
        shift = shift % 128
        return pltpu.roll(value, shift, 1) if shift else value

    spectra = []
    for channel in range(C):
        group, place = divmod(channel, 5)
        first = jnp.zeros((8, 128), f32)
        for ky in range(6):
            block = roll(rows[ky][:, 128 * group : 128 * group + 128], MZ * (ky - place))
            first = jnp.where(lane >= MZ * ky, block, first)
        value = jnp.concatenate([first, block], axis=1)
        real, imag = value[0:3], value[3:6]
        spectra.append(
            (
                jnp.concatenate([real, real, real[0:2]], axis=0)[None],
                jnp.concatenate([imag, imag, imag[0:2]], axis=0)[None],
            )
        )
    mixed = []
    for start in range(0, C, 5):
        by_real = jnp.zeros((5, 8, 256), f32)
        by_imag = jnp.zeros((5, 8, 256), f32)
        for channel in range(C):
            weight = w_ref[channel, start : start + 5]
            by_real += spectra[channel][0] * weight
            by_imag += spectra[channel][1] * weight
        for place in range(5):
            real = by_real[place, 0:3] - by_imag[place, 3:6]
            imag = by_real[place, 3:6] + by_imag[place, 0:3]
            mixed.append(jnp.concatenate([real, imag], axis=0))
    lane = lane[:6]
    for group in range(GROUPS):
        for ky in range(6):
            tile = jnp.zeros((6, 128), f32)
            for place in range(5):
                value = mixed[5 * group + place]
                block = value[:, :128]
                if ky == 5:
                    rest = value[:, 128:]
                    block = jnp.where(lane >= 120, block, rest)
                block = roll(block, MZ * (place - ky))
                inside = (lane >= MZ * place) & (lane < MZ * place + MZ)
                tile = jnp.where(inside, block, tile)
            for narrow in range(NARROW):
                out_ref[narrow, 6 * ky : 6 * ky + 6, 128 * group : 128 * group + 128] = tile
    for narrow in range(NARROW):
        out_ref[narrow, 36:40, :] = jnp.zeros((4, LANES), f32)


def backward_rows(table_ref, in_ref, out_ref):
    high, low = split(in_ref[...].reshape(-1, LANES))
    part = dot(table_ref[...], jnp.concatenate([high, low, high], axis=0))
    out_ref[...] = part.reshape(out_ref.shape)


def gelu(value):
    return 0.5 * value * (1.0 + lax.erf(value * np.float32(np.sqrt(0.5))))


def linear_cells(
    x_ref, lin_ref, bias_ref, out_ref, x_buf, out_buf, lh_ref, ll_ref, in_sem, out_sem
):
    def fetch(y):
        return pltpu.make_async_copy(x_ref.at[:, y], x_buf.at[y], in_sem.at[y])

    def leave(y):
        return pltpu.make_async_copy(out_buf.at[y], out_ref.at[:, y], out_sem.at[y])

    for y in range(16):
        fetch(y).start()
    spread = lax.broadcasted_iota(jnp.int32, (160, C), 0) // 8
    spread = (spread == lax.broadcasted_iota(jnp.int32, (160, C), 1)).astype(bf16)
    rows = lax.broadcasted_iota(jnp.int32, (160, 160), 0)
    cols = lax.broadcasted_iota(jnp.int32, (160, 160), 1)
    same = (rows & 7) == (cols & 7)
    for part, ref in zip(split(lin_ref[...]), (lh_ref, ll_ref)):
        wide = dot(spread, part, ((1,), (1,))).astype(bf16)
        wide = dot(wide, spread, ((1,), (1,)))
        ref[...] = jnp.where(same, wide, 0.0).astype(bf16)

    def row_step(y, carry):
        fetch(y).wait()
        for block in range(4):
            at = slice(8 * block, 8 * block + 8)
            cells = split(x_buf[y, :, at, :].reshape(C * 8, N))
            linear = dot3((lh_ref[...], ll_ref[...]), cells).reshape(C, 8, N)
            for channel in range(C):
                out_buf[y, channel, at, :] = linear[channel] + bias_ref[0, channel]
        leave(y).start()
        return carry

    lax.fori_loop(0, 16, row_step, 0)
    for y in range(16):
        leave(y).wait()


def backward_cells(
    linear_ref, in_ref, table_ref, phase_ref, out_ref,
    x_buf, in_buf, out_buf, cell_ref, x_sem, in_sem, out_sem,
):
    def modes_in(half):
        at = pl.ds(48 * half, 48)
        return pltpu.make_async_copy(in_ref.at[:, at], in_buf.at[:, at], in_sem.at[half])

    def fetch(y):
        return pltpu.make_async_copy(linear_ref.at[:, y], x_buf.at[y], x_sem.at[y])

    def leave(y):
        return pltpu.make_async_copy(out_buf.at[y], out_ref.at[:, y], out_sem.at[y])

    modes_in(0).start()
    for tile in range(5):
        cell_ref[tile, SEQS * 8 :, :] = jnp.zeros((512 - SEQS * 8, 128), f32)

    def half_step(half, carry):
        modes_in(half).wait()

        @pl.when(half == 0)
        def _():
            for y in range(AHEAD):
                fetch(y).start()
            modes_in(1).start()

        base = 48 * half
        turn = phase_ref[lax.axis_index("narrow")]
        turn_c, turn_s = turn[0:1], turn[1:2]
        last = None
        for group in range(GROUPS):
            lanes = slice(128 * group, 128 * group + 128)

            def mode(index, part):
                at = base + 16 * (index % 3) + 8 * part
                return in_buf[index // 3, pl.ds(pl.multiple_of(at, 8), 8), lanes]

            first, second = [], []
            for freq in range(HALF + 1):
                if freq == 0:
                    u, v = mode(0, 0), mode(0, 1)
                elif freq == HALF:
                    u, v = mode(48 - freq, 0), mode(48 - freq, 1)
                else:
                    u = mode(freq, 0) + mode(48 - freq, 0)
                    v = mode(freq, 1) + mode(48 - freq, 1)
                first.append(u)
                second.append(v)
            for freq in range(1, HALF + 1):
                if freq == HALF:
                    u, v = mode(48 - freq, 1), -mode(48 - freq, 0)
                else:
                    u = mode(48 - freq, 1) - mode(freq, 1)
                    v = mode(freq, 0) - mode(48 - freq, 0)
                first.append(u)
                second.append(v)
            u, v = jnp.concatenate(first, axis=0), jnp.concatenate(second, axis=0)
            u, v = turn_c * u - turn_s * v, turn_s * u + turn_c * v
            cells = dot3(
                split(jnp.concatenate([u, v], axis=1)),
                (window_of(table_ref, group), window_of(table_ref, group, 352)),
                ((1,), (1,)),
            )
            left, right = cells[:, :128], cells[:, 128:]
            cell_ref[group, : SEQS * 8, :] = left if last is None else left + last
            last = right
        cell_ref[GROUPS, : SEQS * 8, :] = last

        def row_step(row, carry):
            y = 8 * half + row
            seqs = jnp.concatenate(
                [cell_ref[tile, pl.ds(row, 64, stride=8), :] for tile in range(5)], axis=1
            )
            pair = jnp.transpose(jnp.concatenate(split(seqs), axis=0))
            spatial = dot(jnp.concatenate([pair, pair], axis=1), table_ref[704:960])
            fetch(y).wait()

            @pl.when(y + AHEAD < 16)
            def _():
                fetch(y + AHEAD).start()

            out_buf[y] = gelu(x_buf[y] + spatial.reshape(C, 32, N))
            leave(y).start()
            return carry

        lax.fori_loop(0, 8, row_step, 0)
        return carry

    lax.fori_loop(0, 2, half_step, 0)
    for y in range(16):
        leave(y).wait()


def whole(shape):
    return pl.BlockSpec(shape, lambda *_: (0,) * len(shape))


def params(mib):
    return pltpu.CompilerParams(
        dimension_semantics=("arbitrary",), vmem_limit_bytes=mib * 1024 * 1024
    )


def cells_forward(field):
    eh, el = halves(x_table())
    zh, zl = halves(z_table(1.0))
    vmem = pl.BlockSpec(memory_space=pltpu.VMEM)
    return pl.pallas_call(
        forward_cells,
        in_specs=[pl.BlockSpec(memory_space=pl.ANY), vmem, vmem, vmem, vmem],
        out_specs=pl.BlockSpec(memory_space=pl.ANY),
        out_shape=jax.ShapeDtypeStruct((WIDE, 96, LANES), f32),
        scratch_shapes=[
            pltpu.VMEM((16, C, 32, N), f32),
            pltpu.VMEM((WIDE, 96, LANES), f32),
            pltpu.VMEM((5, 512, 128), f32),
            pltpu.SemaphoreType.DMA((16,)),
            pltpu.SemaphoreType.DMA((2,)),
        ],
        compiler_params=pltpu.CompilerParams(vmem_limit_bytes=60 * 1024 * 1024),
        name="forward_cells",
    )(
        field,
        np.concatenate([eh, el]),
        zh,
        zl,
        phase_table(),
    )


def rows_forward(moved):
    high, low = halves(y_tables()[0])
    return pl.pallas_call(
        forward_rows,
        out_shape=jax.ShapeDtypeStruct((NARROW, ROWS, LANES), f32),
        compiler_params=pltpu.CompilerParams(vmem_limit_bytes=32 * 1024 * 1024),
        name="forward_rows",
    )(high, low, moved)


def arrange_weights(spec_weight):
    return pl.pallas_call(
        arrange,
        grid=(4,),
        in_specs=[pl.BlockSpec((2, 5, C, 3, 144), lambda i: (0, i, 0, 0, 0))],
        out_specs=pl.BlockSpec((5, C, 8, 256), lambda i: (i, 0, 0, 0)),
        out_shape=jax.ShapeDtypeStruct((C, C, 8, 256), f32),
        compiler_params=params(32),
        name="arrange",
    )(spec_weight.reshape(2, C, C, 3, 144))


def mix_modes(moved, weights):
    return pl.pallas_call(
        mix,
        out_shape=jax.ShapeDtypeStruct((NARROW, ROWS, LANES), f32),
        compiler_params=pltpu.CompilerParams(vmem_limit_bytes=32 * 1024 * 1024),
        name="mix",
    )(moved, weights)


def rows_backward(moved):
    high, low = halves(y_tables()[1])
    return pl.pallas_call(
        backward_rows,
        grid=(2,),
        in_specs=[
            pl.BlockSpec((768, 3 * NARROW * ROWS), lambda s: (s, 0)),
            whole((NARROW, ROWS, LANES)),
        ],
        out_specs=pl.BlockSpec((8, 96, LANES), lambda s: (s, 0, 0)),
        out_shape=jax.ShapeDtypeStruct((WIDE, 96, LANES), f32),
        compiler_params=params(32),
        name="backward_rows",
    )(np.concatenate([high, high, low], axis=1), moved)


def linear_part(field, lin_weight, bias):
    return pl.pallas_call(
        linear_cells,
        in_specs=[
            pl.BlockSpec(memory_space=pl.ANY),
            pl.BlockSpec(memory_space=pltpu.VMEM),
            pl.BlockSpec(memory_space=pltpu.SMEM),
        ],
        out_specs=pl.BlockSpec(memory_space=pl.ANY),
        out_shape=jax.ShapeDtypeStruct(field.shape, f32),
        scratch_shapes=[
            pltpu.VMEM((16, C, 32, N), f32),
            pltpu.VMEM((16, C, 32, N), f32),
            pltpu.VMEM((160, 160), bf16),
            pltpu.VMEM((160, 160), bf16),
            pltpu.SemaphoreType.DMA((16,)),
            pltpu.SemaphoreType.DMA((16,)),
        ],
        compiler_params=pltpu.CompilerParams(vmem_limit_bytes=40 * 1024 * 1024),
        cost_estimate=pl.CostEstimate(
            flops=2 * 3 * 160 * field.size, bytes_accessed=8 * field.size, transcendentals=0
        ),
        name="linear_cells",
    )(field, lin_weight.reshape(C, C), bias)


def cells_backward(linear, moved):
    eh, el = halves(x_table() / N)
    scale = np.where(np.arange(MZ) == 0, 1.0, 2.0) / N
    table = z_table(scale)
    table[:, 128:] *= -1
    zh, zl = halves(table)
    vmem = pl.BlockSpec(memory_space=pltpu.VMEM)
    hbm = pl.BlockSpec(memory_space=pl.ANY)
    return pl.pallas_call(
        backward_cells,
        in_specs=[hbm, hbm, vmem, vmem],
        out_specs=hbm,
        out_shape=jax.ShapeDtypeStruct(linear.shape, f32),
        scratch_shapes=[
            pltpu.VMEM((16, C, 32, N), f32),
            pltpu.VMEM((WIDE, 96, LANES), f32),
            pltpu.VMEM((16, C, 32, N), f32),
            pltpu.VMEM((5, 512, 128), f32),
            pltpu.SemaphoreType.DMA((16,)),
            pltpu.SemaphoreType.DMA((2,)),
            pltpu.SemaphoreType.DMA((16,)),
        ],
        compiler_params=pltpu.CompilerParams(vmem_limit_bytes=46 * 1024 * 1024),
        name="backward_cells",
    )(linear, moved, np.concatenate([zh, zl, eh, eh, el, np.zeros_like(el)]), phase_table())


def body(field, spec_weight, lin_weight, bias):
    moved = cells_forward(field)
    moved = lax.all_to_all(moved, "wide", split_axis=0, concat_axis=0, tiled=True)
    moved = rows_forward(moved)
    moved = lax.all_to_all(moved, "narrow", split_axis=0, concat_axis=0, tiled=True)
    moved = mix_modes(moved, arrange_weights(spec_weight))
    moved = lax.all_to_all(moved, "narrow", split_axis=0, concat_axis=0, tiled=True)
    moved = rows_backward(moved)
    moved = lax.all_to_all(moved, "wide", split_axis=0, concat_axis=0, tiled=True)
    linear = linear_part(field, lin_weight, bias)
    return cells_backward(linear, moved)


def solution(mesh):
    placed = (
        P(None, "wide", "narrow", None),
        P(None, None, None, None, "wide", "narrow"),
        P(),
        P(),
    )
    return jax.shard_map(
        body, mesh=mesh, in_specs=placed, out_specs=P(None, "wide", "narrow", None), check_vma=False
    )
```
